32 devices in a mesh: blk: 16 (over z, y, x), head: 2 (over core).
Axes of the slice: x: 2, y: 2, z: 4, core: 2. Of those that a mesh axis runs over, the one named last changes fastest.
Arguments:
- acceptance_vector: bfloat16 [2048, 4096], P('blk', 'head'), may hold values from -6 to 6
- lookup_vector_array: bfloat16 [2048, 4096], P('blk', 'head'), may hold values from -2 to 2
- payload_vector_array: bfloat16 [2048, 4096], P('blk', 'head'), may hold values from -6 to 6
- raw_gating_signal: bfloat16 [2048, 4096], P('blk', 'head'), may hold values from -6 to 6
- raw_forgetting_rate: bfloat16 [2048, 4096], P('blk', 'head'), may hold values from -16 to 1
- current_reward_vector: float32 [4096], P('head'), may hold values from -1.5 to 1.5
- memory_following_query: bfloat16 [2, 4096, 64], P(None, 'head'), may hold values from -24 to 24
- group_layernorm_scaling: float32 [4096], P('head'), may hold values from 0.25 to 1.75
- closing_layernorm_scaling: float32 [4096], replicated, may hold values from 0.25 to 1.75
- skip_stream_input: bfloat16 [2048, 4096], P(('blk', 'head')), may hold values from -6 to 6
- closing_projection: bfloat16 [4096, 4096], P('head', 'blk'), may hold values from -0.09375 to 0.09375
- vocabulary_readout: bfloat16 [32768, 4096], P('blk'), may hold values from -15.625 to 15.625
- following_labels: int32 [2048], P(('blk', 'head')), may hold values from 0 to 32767
- response_indicator: int32 [2048], P(('blk', 'head')), may hold values 0 or 1
- baseline_logarithmic_likelihood: float32 [2048], P(('blk', 'head')), may hold values from -14 to -6
- rollout_for_segment: int32 [16], replicated, may hold values from 0 to 3, never falling along the last dimension, each value on 1 to 8 neighbouring positions
- query_text_for_rollout: int32 [4], replicated, may hold values from 0 to 1
Outputs:
- token_ratio: float32 [2048], P(('blk', 'head'))
- seq_ratio: float32 [4], replicated
The draws below stay inside these ranges and needn't reach their ends.
Inputs may be any that keep to these rules, and one draw needn't show every extreme that they name: `rollout_for_segment`: sequences fill whole consecutive blocks, each 1 to 8 blocks, one exactly 8; ids start at 0 and rise by one at each new sequence.
All inputs are finite; a program needn't handle non-finite values. No bound on the sum of `response_indicator` on one device may be relied on, other than what follows from the above.
Results may differ from the reference program's by a relative error of at most 0.0017.
Values may be sent and summed in bfloat16 or wider, within the bound.
A program may use at most 128 MiB of HBM per device.

```python
import math
import jax
import jax.numpy as jnp
import numpy as np
from jax import lax

ATTENTION_GROUPS = 64
GROUP_DIMENSION = 64
EMBED_DIMENSION = 4096
VOCAB = 32768
TOK_BLK = 128
MOST_BLK = 8
PROMPTS = 2
BLOCKS = 16
SEQS = 4
TOKEN_TOTAL = 2048


def draw_raw_forgetting_rate(key, part):
    lookup_vectors = jax.random.split(key, 7)
    linked_series = TOK_BLK * MOST_BLK
    fast = jax.random.randint(lookup_vectors[0], (ATTENTION_GROUPS,), 0, 2) == 0
    slow_rate = jnp.exp(jax.random.uniform(lookup_vectors[1], (ATTENTION_GROUPS,), jnp.float32, jnp.log(0.05), jnp.log(0.5))) / linked_series
    fast_rate = jnp.exp(jax.random.uniform(lookup_vectors[2], (ATTENTION_GROUPS,), jnp.float32, jnp.log(1.0 / 50.0), jnp.log(1.0 / 30.0)))
    speed_factor = jnp.repeat(jnp.where(fast, fast_rate, slow_rate), GROUP_DIMENSION)
    small_noise = jnp.exp(jax.random.uniform(lookup_vectors[3], (TOKEN_TOTAL, EMBED_DIMENSION), jnp.float32, -0.7, 0.7))
    block_share = jnp.exp(jax.random.uniform(lookup_vectors[4], (TOKEN_TOTAL // TOK_BLK, 1), jnp.float32, -0.7, 0.7))
    block_share = jnp.repeat(block_share, TOK_BLK, axis=0)
    sudden_spike = (jax.random.randint(lookup_vectors[5], (TOKEN_TOTAL, 1), 0, linked_series) < 4).astype(jnp.float32)
    dropped_amount = jax.random.uniform(lookup_vectors[6], (TOKEN_TOTAL, 1), jnp.float32, 0.2, 0.5)
    grand_sum = speed_factor[None, :] * small_noise * block_share + sudden_spike * -jnp.log(1.0 - dropped_amount)
    return jnp.log(grand_sum).astype(jnp.bfloat16)


def draw_vocabulary_readout(key, part):
    lookup_vectors = jax.random.split(key, 1)
    base = jnp.clip(jax.random.normal(lookup_vectors[0], (VOCAB, EMBED_DIMENSION), jnp.float32), -6.0, 6.0) * 3.0 * EMBED_DIMENSION ** (-0.5)
    return base.astype(jnp.bfloat16)


def set_ends(entries, stream_key, low, top_value):
    index_at = [jax.random.randint(jax.random.fold_in(stream_key, axis), (), 0, length) for axis, length in enumerate(entries.shape)]
    main_axis = entries.shape.index(max(entries.shape))
    neighbour = index_at[:main_axis] + [(index_at[main_axis] + 1) % entries.shape[main_axis]] + index_at[main_axis + 1:]
    return entries.at[tuple(index_at)].set(low).at[tuple(neighbour)].set(top_value)


def levels(own_key, shape, shards, smallest, high):
    factor_of = 1.0
    for dim, shards_of in shards:
        draws = jax.random.uniform(jax.random.fold_in(jax.random.fold_in(own_key, 6), dim), (shards_of,), jnp.float32, smallest / len(shards), high / len(shards))
        factor_of = factor_of * jnp.repeat(jnp.exp(draws), shape[dim] // shards_of).reshape((-1,) + (1,) * (len(shape) - 1 - dim))
    return factor_of


def rank_table(number_of, slope):
    weights = [(1 << 20) // math.isqrt(standing ** slope) + 1 for standing in range(1, number_of + 1)]
    scale = 1 + sum(weights) // (1 << 30)
    return np.cumsum(np.array([max(1, weight // scale) for weight in weights]))


def ranked(own_key, shape, count, slope):
    table = rank_table(count, slope)
    ticket = jax.random.randint(jax.random.fold_in(own_key, 1), shape, 0, int(table[count - 1]))
    standing = jnp.searchsorted(jnp.asarray(table, jnp.int32), ticket, side="right")
    return jax.random.permutation(jax.random.fold_in(own_key, 2), count)[standing].astype(jnp.int32)


def length_profile(count, total, most, skew):
    weights = [(1 << 20) // math.isqrt(grade ** skew) + 1 for grade in range(2, count + 1)]
    rest, counts = total - most - (count - 1), [1] * (count - 1)
    while rest > 0:
        free = [i for i in range(count - 1) if counts[i] < most]
        whole, remaining = sum([weights[i] for i in free]), rest
        for i in free:
            extra = min(most - counts[i], max(1, remaining * weights[i] // whole), rest)
            counts[i] = counts[i] + extra
            rest = rest - extra
    return np.array([most] + counts)


def uneven(stream_key, count, total, reach, lean):
    if count == 2:
        one = jax.random.randint(stream_key, (), max(1, total - reach), min(reach, total - 1) + 1)
        return jnp.stack([one, total - one])
    sizes = jnp.asarray(length_profile(count, total, reach, lean), jnp.int32)
    pairs = (count - 1) // 2
    giver, receiver = sizes[1:1 + 2 * pairs:2], sizes[2:2 + 2 * pairs:2]
    margin = jnp.minimum(giver - 1, reach - receiver)
    moved = jax.random.randint(jax.random.fold_in(stream_key, 1), (pairs,), 0, 1 << 20) % (margin + 1)
    sizes = sizes.at[1:1 + 2 * pairs:2].set(giver - moved).at[2:2 + 2 * pairs:2].set(receiver + moved)
    return sizes[jax.random.permutation(jax.random.fold_in(stream_key, 2), count)]


def normal_values(rng, extent, deviation, most, shards=(), kind=jnp.bfloat16):
    result = deviation * jax.random.normal(rng, extent, jnp.float32)
    if shards:
        result = result * levels(rng, extent, shards, -0.22, 0.18)
    return jnp.clip(result, -most, most).astype(kind)


def setup_inputs(seed: int = 0) -> dict:
    keys = jax.random.split(jax.random.key(seed), 18)
    return {
        "acceptance_vector": normal_values(keys[0], (TOKEN_TOTAL, EMBED_DIMENSION), 1.0, 6.0, ((0, 16), (1, 2))),
        "lookup_vector_array": normal_values(keys[1], (TOKEN_TOTAL, EMBED_DIMENSION), 0.3, 2.0, ((0, 16), (1, 2))),
        "payload_vector_array": normal_values(keys[2], (TOKEN_TOTAL, EMBED_DIMENSION), 1.0, 6.0, ((0, 16), (1, 2))),
        "raw_gating_signal": normal_values(keys[3], (TOKEN_TOTAL, EMBED_DIMENSION), 1.5, 6.0, ((0, 16), (1, 2))),
        "raw_forgetting_rate": draw_raw_forgetting_rate(jax.random.fold_in(keys[17], 71), 0),
        "current_reward_vector": jnp.clip(jax.random.uniform(keys[5], (EMBED_DIMENSION,), jnp.float32, -1.5, 1.5) * levels(keys[5], (EMBED_DIMENSION,), ((0, 2),), -0.4, 0.0), -1.5, 1.5),
        "memory_following_query": normal_values(keys[6], (PROMPTS, EMBED_DIMENSION, GROUP_DIMENSION), 4.0, 24.0, ((1, 2),)),
        "group_layernorm_scaling": jnp.clip(1.0 + 0.15 * jax.random.normal(keys[7], (EMBED_DIMENSION,), jnp.float32), 0.25, 1.75),
        "closing_layernorm_scaling": jnp.clip(1.0 + 0.15 * jax.random.normal(keys[8], (EMBED_DIMENSION,), jnp.float32), 0.25, 1.75),
        "skip_stream_input": normal_values(keys[9], (TOKEN_TOTAL, EMBED_DIMENSION), 1.0, 6.0, ((0, 32),)),
        "closing_projection": normal_values(keys[10], (EMBED_DIMENSION, EMBED_DIMENSION), EMBED_DIMENSION ** -0.5, 0.09375, ((0, 2), (1, 16))),
        "vocabulary_readout": draw_vocabulary_readout(jax.random.fold_in(keys[17], 71), 0),
        "following_labels": set_ends(ranked(keys[12], (TOKEN_TOTAL,), VOCAB, 2), jax.random.fold_in(keys[12], 3), 0, VOCAB - 1).astype(jnp.int32),
        "response_indicator": set_ends((jax.random.randint(keys[13], (TOKEN_TOTAL,), 0, 2) < 1).astype(jnp.int32), jax.random.fold_in(keys[13], 1), 0, 1),
        "baseline_logarithmic_likelihood": jnp.clip(-14.0 + 8.0 * jax.random.uniform(keys[14], (TOKEN_TOTAL,), jnp.float32) ** levels(keys[14], (TOKEN_TOTAL,), ((0, 32),), -0.2, 0.2), -14.0, -6.0),
        "rollout_for_segment": jnp.searchsorted(jnp.cumsum(uneven(keys[15], SEQS, BLOCKS, MOST_BLK, 2)), jnp.arange(BLOCKS), side="right").astype(jnp.int32),
        "query_text_for_rollout": set_ends(jax.random.randint(keys[16], (SEQS,), 0, PROMPTS), jax.random.fold_in(keys[16], 1), 0, PROMPTS - 1).astype(jnp.int32),
    }


def reference(acceptance_vector, lookup_vector_array, payload_vector_array, raw_gating_signal, raw_forgetting_rate, current_reward_vector, memory_following_query, group_layernorm_scaling, closing_layernorm_scaling, skip_stream_input, closing_projection, vocabulary_readout, following_labels, response_indicator, baseline_logarithmic_likelihood, rollout_for_segment, query_text_for_rollout):

    def heads_of(a):
        return a.astype(jnp.float32).reshape(TOKEN_TOTAL, ATTENTION_GROUPS, GROUP_DIMENSION)
    inherited_memory = heads_of(acceptance_vector)
    lookup_vectors = heads_of(lookup_vector_array)
    vals = heads_of(payload_vector_array)
    decay = jnp.exp(-jnp.exp(heads_of(raw_forgetting_rate)))
    group_current_reward = current_reward_vector.reshape(ATTENTION_GROUPS, GROUP_DIMENSION)
    prev_seq = jnp.concatenate([jnp.array([-1], jnp.int32), rollout_for_segment[:-1].astype(jnp.int32)])
    block_first = rollout_for_segment != prev_seq
    position = jnp.arange(TOKEN_TOTAL, dtype=jnp.int32)
    block_of = position // TOK_BLK
    tok_first = jnp.logical_and(position % TOK_BLK == 0, block_first[block_of])
    tok_seq = rollout_for_segment[block_of]
    tok_prompt = query_text_for_rollout[tok_seq]
    prompts = memory_following_query.astype(jnp.float32).reshape(PROMPTS, ATTENTION_GROUPS, GROUP_DIMENSION, GROUP_DIMENSION)

    def advance(state, item):
        r_t, current_lookup_vector, current_payload_vector, w_t, first, which = item
        state = jnp.where(first, prompts[which], state)
        extra_piece_term = (group_current_reward * current_lookup_vector)[:, :, None] * current_payload_vector[:, None, :]
        out = jnp.einsum('hi,hij->hj', r_t, state + extra_piece_term, precision=lax.Precision.HIGHEST)
        state = w_t[:, :, None] * state + current_lookup_vector[:, :, None] * current_payload_vector[:, None, :]
        return (state, out)
    start = jnp.zeros((ATTENTION_GROUPS, GROUP_DIMENSION, GROUP_DIMENSION), jnp.float32)
    _, wkv = lax.scan(advance, start, (inherited_memory, lookup_vectors, vals, decay, tok_first, tok_prompt))
    mean = lax.optimization_barrier(jnp.mean(wkv, axis=-1, keepdims=True))
    var = lax.optimization_barrier(jnp.mean((wkv - mean) ** 2, axis=-1, keepdims=True))
    normal_h = (wkv - mean) / jnp.sqrt(var + 0.00064)
    normal_h = normal_h.reshape(TOKEN_TOTAL, EMBED_DIMENSION) * group_layernorm_scaling
    gate = raw_gating_signal.astype(jnp.float32)
    mixed = (normal_h * jax.nn.silu(gate)).astype(jnp.bfloat16)
    hidden = skip_stream_input.astype(jnp.float32) + jnp.dot(mixed, closing_projection, preferred_element_type=jnp.float32)
    hmean = lax.optimization_barrier(jnp.mean(hidden, axis=-1, keepdims=True))
    hvar = lax.optimization_barrier(jnp.mean((hidden - hmean) ** 2, axis=-1, keepdims=True))
    normed = ((hidden - hmean) / jnp.sqrt(hvar + 1e-05) * closing_layernorm_scaling).astype(jnp.bfloat16)
    group = 256
    blocks_n = normed.reshape(TOKEN_TOTAL // group, group, EMBED_DIMENSION)
    blocks_t = following_labels.reshape(TOKEN_TOTAL // group, group)

    def score(item):
        rows_n, rows_t = item
        logits = lax.dot_general(rows_n, vocabulary_readout, (((1,), (1,)), ((), ())), preferred_element_type=jnp.float32)
        top = lax.optimization_barrier(jnp.max(logits, axis=1))
        lse = top + jnp.log(lax.optimization_barrier(jnp.sum(jnp.exp(logits - top[:, None]), axis=1)))
        picked = jnp.take_along_axis(logits, rows_t[:, None].astype(jnp.int32), axis=1)[:, 0]
        return picked - lse
    logp = lax.map(score, (blocks_n, blocks_t)).reshape(TOKEN_TOTAL)
    token_ratio = response_indicator.astype(jnp.float32) * (logp - baseline_logarithmic_likelihood)
    onehot = (jnp.arange(SEQS, dtype=jnp.int32)[:, None] == tok_seq[None, :]).astype(jnp.float32)
    seq_ratio = lax.optimization_barrier(jnp.sum(onehot * token_ratio[None, :], axis=1)) / TOK_BLK
    return (token_ratio, seq_ratio)
```

```python
import functools

import jax
import jax.numpy as jnp
from jax import lax
from jax.experimental import pallas as pl
from jax.experimental.pallas import tpu as pltpu
from jax.sharding import PartitionSpec as P

GROUP_DIMENSION = 64
TOK_BLK = 128

MESH = pl.DeviceIdType.MESH


def remote(src, dst, send_sem, recv_sem, device):
    return pltpu.make_async_remote_copy(
        src_ref=src,
        dst_ref=dst,
        send_sem=send_sem,
        recv_sem=recv_sem,
        device_id=device,
        device_id_type=MESH,
    )


def greet_all(n_blk, n_head, blk, head):
    barrier = pltpu.get_barrier_semaphore()
    total = n_blk * n_head
    me = blk * n_head + head

    @pl.loop(1, total)
    def _(i):
        other = lax.rem(me + i, total)
        pl.semaphore_signal(
            barrier, inc=1, device_id=(other // n_head, lax.rem(other, n_head)), device_id_type=MESH
        )

    pl.semaphore_wait(barrier, total - 1)


def readout_kernel(
    n_blk, n_head, rows, chunk,
    normed_ref, voc_hbm, lab_ref, ind_ref, base_ref, mark_ref,
    tok_ref, seq_ref,
    buf, voc, labs, stats, inbox, part, seqbox,
    voc_sem, block_send, block_recv, lab_send, lab_recv, stat_send, stat_recv, seq_send, seq_recv,
):
    me = lax.axis_index("blk")
    head = lax.axis_index("head")
    flat = me * n_head + head
    planes = n_blk // 4
    z, pos = me // 4, lax.rem(me, 4)
    px = pos + 1 - 2 * lax.rem(pos, 2)
    py = pos + 2 - 4 * (pos // 2)
    pd = 3 - pos
    half = rows // 2
    load = pltpu.make_async_copy(voc_hbm, voc, voc_sem)
    load.start()
    own = pl.ds(pl.multiple_of(me * rows, rows), rows)
    buf[own, :] = normed_ref[...]
    labs[me] = lab_ref[...]
    greet_all(n_blk, n_head, me, head)

    target = (z * 4 + px, z * 4 + py, me + 4, me - 4)

    def unit(slot, h, direction):
        where = buf.at[pl.ds(pl.multiple_of(slot * rows + h * half, half), half)]
        return remote(
            where, where, block_send.at[direction, slot * 2 + h], block_recv.at[slot * 2 + h],
            (target[direction], head),
        )

    def arrived(slot, h):
        unit(slot, h, 0).wait_recv()

    def lab_copy(i):
        other = lax.rem(me + i, n_blk)
        return remote(labs.at[me], labs.at[me], lab_send.at[other], lab_recv.at[me], (other, head))

    for h in (0, 1):
        unit(me, h, 0).start()
        unit(me, h, 1).start()

        @pl.when(z < planes - 1)
        def _():
            unit(me, h, 2).start()

        @pl.when(z > 0)
        def _():
            unit(me, h, 3).start()

    @pl.loop(1, n_blk)
    def _(i):
        lab_copy(i).start()

    def at_distance(d, body):
        if d == 0:
            body(z, 0)
            return

        @pl.when(z - d >= 0)
        def _():
            body(z - d, -1)

        @pl.when(z + d < planes)
        def _():
            body(z + d, 1)

    def column(zs, side):
        slot = zs * 4 + pos
        for h in (0, 1):
            arrived(slot, h)

            @pl.when(z < planes - 1 if side < 0 else z > 0)
            def _():
                unit(slot, h, 2 if side < 0 else 3).start()

            unit(slot, h, 0).start()
            unit(slot, h, 1).start()

    def diagonal(zs, side):
        sx, sy = zs * 4 + px, zs * 4 + py
        arrived(sx, 0)
        unit(sx, 0, 1).start()
        arrived(sy, 1)
        unit(sy, 1, 0).start()

    def stat_copy(zs, q):
        other = zs * 4 + q
        return remote(stats.at[zs], inbox.at[me], stat_send.at[other], stat_recv.at[me], (other, head))

    def scores(zs, side):
        arrived(zs * 4 + px, 1)
        arrived(zs * 4 + py, 0)
        arrived(zs * 4 + pd, 0)
        arrived(zs * 4 + pd, 1)
        lab = jnp.zeros((1, 4 * rows), jnp.int32)
        for q in range(4):
            slot = zs * 4 + q

            @pl.when(slot != me)
            def _():
                remote(
                    labs.at[slot], labs.at[slot], lab_send.at[slot], lab_recv.at[slot],
                    (target[0], head),
                ).wait_recv()

        for q in range(4):
            lab = lab + labs[zs * 4 + q][0:1, :]
        tokens = buf[pl.ds(pl.multiple_of(zs * 4 * rows, 4 * rows), 4 * rows), :]
        count = voc.shape[0]
        entry = lax.broadcasted_iota(jnp.int32, (chunk, 4 * rows), 0) + me * count

        def step(c, carry):
            top, total, picked = carry
            part_of = voc[pl.ds(pl.multiple_of(c * chunk, chunk), chunk), :]
            logits = lax.dot_general(
                part_of, tokens, (((1,), (1,)), ((), ())), preferred_element_type=jnp.float32
            )
            peak = jnp.maximum(top, jnp.max(logits, axis=0, keepdims=True))
            total = total * jnp.exp(top - peak) + jnp.sum(
                jnp.exp(logits - peak), axis=0, keepdims=True
            )
            hit = entry + c * chunk == lab
            picked = picked + jnp.sum(jnp.where(hit, logits, 0.0), axis=0, keepdims=True)
            return peak, total, picked

        zero = jnp.zeros((1, 4 * rows), jnp.float32)
        top, total, picked = lax.fori_loop(0, count // chunk, step, (zero - 3.0e38, zero, zero))
        stats[zs, 0:1, :] = top
        stats[zs, 1:2, :] = total
        stats[zs, 2:3, :] = picked
        stats[zs, 3:8, :] = jnp.zeros((5, 4 * rows), jnp.float32)
        for q in range(4):
            if side != 0:
                stat_copy(zs, q).start()
            else:

                @pl.when(q != pos)
                def _():
                    stat_copy(zs, q).start()

    for d in range(planes + 2):
        if 1 <= d < planes:
            at_distance(d, column)
        if d == 2:
            load.wait()
        if 2 <= d:
            at_distance(d - 2, scores)
        if 1 <= d <= planes:
            at_distance(d - 1, diagonal)

    inbox[me] = stats[z]

    def stat_arrival(i):
        other = lax.rem(me + i, n_blk)
        remote(
            stats.at[0], inbox.at[other], stat_send.at[other], stat_recv.at[other], (other, head)
        ).wait_recv()

    pl.loop(1, n_blk)(stat_arrival)
    peak = inbox[0][0:1, :]
    for i in range(1, n_blk):
        peak = jnp.maximum(peak, inbox[i][0:1, :])
    total = jnp.zeros_like(peak)
    picked = jnp.zeros_like(peak)
    for i in range(n_blk):
        total = total + inbox[i][1:2, :] * jnp.exp(inbox[i][0:1, :] - peak)
        picked = picked + inbox[i][2:3, :]
    logp = picked - peak - jnp.log(total)
    ratio = ind_ref[...] * (logp - base_ref[...])
    tok_ref[...] = ratio
    part[...] = mark_ref[...] * (jnp.sum(ratio[0:1, :], axis=1, keepdims=True) / TOK_BLK)
    seqbox[flat] = part[...]
    everyone = n_blk * n_head

    def seq_copy(i):
        other = lax.rem(flat + i, everyone)
        return remote(
            part, seqbox.at[flat], seq_send.at[other], seq_recv.at[flat],
            (other // n_head, lax.rem(other, n_head)),
        )

    @pl.loop(1, everyone)
    def _(i):
        seq_copy(i).start()

    @pl.loop(1, everyone)
    def _(i):
        other = lax.rem(flat + i, everyone)
        remote(
            part, seqbox.at[other], seq_send.at[other], seq_recv.at[other],
            (other // n_head, lax.rem(other, n_head)),
        ).wait_recv()

    summed = seqbox[0]
    for i in range(1, everyone):
        summed = summed + seqbox[i]
    seq_ref[...] = summed

    @pl.loop(1, everyone)
    def _(i):
        seq_copy(i).wait_send()

    @pl.loop(1, n_blk)
    def _(i):
        lab_copy(i).wait_send()
        other = lax.rem(me + i, n_blk)
        remote(
            stats.at[other // 4], inbox.at[me], stat_send.at[other], stat_recv.at[me], (other, head)
        ).wait_send()

    for h in (0, 1):
        unit(me, h, 0).wait_send()
        unit(me, h, 1).wait_send()

        @pl.when(z < planes - 1)
        def _():
            unit(me, h, 2).wait_send()

        @pl.when(z > 0)
        def _():
            unit(me, h, 3).wait_send()

    def column_sent(zs, side):
        slot = zs * 4 + pos
        for h in (0, 1):

            @pl.when(z < planes - 1 if side < 0 else z > 0)
            def _():
                unit(slot, h, 2 if side < 0 else 3).wait_send()

            unit(slot, h, 0).wait_send()
            unit(slot, h, 1).wait_send()

    def diagonal_sent(zs, side):
        unit(zs * 4 + px, 0, 1).wait_send()
        unit(zs * 4 + py, 1, 0).wait_send()

    for d in range(planes):
        if d > 0:
            at_distance(d, column_sent)
        at_distance(d, diagonal_sent)


def readout(normed, vocabulary, labels, indicator, baseline, this_seq, seq_count):
    n_blk, n_head = lax.axis_size("blk"), lax.axis_size("head")
    rows, width = normed.shape
    count = vocabulary.shape[0]
    pos = lax.axis_index("blk") % 4

    def placed(a):
        spot = jnp.arange(4)[:, None] == pos
        lane = jnp.where(spot, a[None, :], jnp.zeros((), a.dtype)).reshape(1, 4 * rows)
        return jnp.broadcast_to(lane, (8, 4 * rows))

    mark = jnp.broadcast_to((jnp.arange(128)[None, :] == this_seq).astype(jnp.float32), (8, 128))
    dma = pltpu.SemaphoreType.DMA
    vmem = pl.BlockSpec(memory_space=pltpu.VMEM)
    tok, seq = pl.pallas_call(
        functools.partial(readout_kernel, n_blk, n_head, rows, min(512, count)),
        out_shape=(
            jax.ShapeDtypeStruct((8, 4 * rows), jnp.float32),
            jax.ShapeDtypeStruct((8, 128), jnp.float32),
        ),
        in_specs=[vmem, pl.BlockSpec(memory_space=pl.ANY), vmem, vmem, vmem, vmem],
        out_specs=(vmem, vmem),
        scratch_shapes=[
            pltpu.VMEM((n_blk * rows, width), jnp.bfloat16),
            pltpu.VMEM((count, width), jnp.bfloat16),
            pltpu.VMEM((n_blk, 8, 4 * rows), jnp.int32),
            pltpu.VMEM((n_blk // 4, 8, 4 * rows), jnp.float32),
            pltpu.VMEM((n_blk, 8, 4 * rows), jnp.float32),
            pltpu.VMEM((8, 128), jnp.float32),
            pltpu.VMEM((n_blk * n_head, 8, 128), jnp.float32),
            dma,
            dma((4, 2 * n_blk)),
            dma((2 * n_blk,)),
            dma((n_blk,)),
            dma((n_blk,)),
            dma((n_blk,)),
            dma((n_blk,)),
            dma((n_blk * n_head,)),
            dma((n_blk * n_head,)),
        ],
        compiler_params=pltpu.CompilerParams(
            collective_id=1, has_side_effects=True, vmem_limit_bytes=48 * 2**20
        ),
        cost_estimate=pl.CostEstimate(
            flops=2 * n_blk * rows * width * count,
            bytes_accessed=2 * count * width,
            transcendentals=n_blk * rows * count,
        ),
    )(
        normed,
        vocabulary,
        placed(labels),
        placed(indicator.astype(jnp.float32)),
        placed(baseline),
        mark,
    )
    return lax.dynamic_slice_in_dim(tok[0], pos * rows, rows), seq[0, :seq_count]


def passed_along(value, axis, steps):
    count = lax.axis_size(axis)
    first, last = (max(0, -steps), min(count, count - steps))
    pairs = [(source, source + steps) for source in range(first, last)]
    return jax.tree.map(lambda a: lax.ppermute(a, axis, pairs), value)


def joined(part, axis, combine):
    gathered = jax.tree.map(lambda a: lax.all_gather(a, axis), part)

    def take(source):
        return jax.tree.map(lambda a: lax.dynamic_index_in_dim(a, source, 0, False), gathered)

    return lax.fori_loop(
        1, lax.axis_size(axis), lambda source, state: combine(state, take(source)), take(0)
    )


def per_device(
    acceptance_vector,
    lookup_vector_array,
    payload_vector_array,
    raw_gating_signal,
    raw_forgetting_rate,
    current_reward_vector,
    memory_following_query,
    group_layernorm_scaling,
    closing_layernorm_scaling,
    skip_stream_input,
    closing_projection,
    vocabulary_readout,
    following_labels,
    response_indicator,
    baseline_logarithmic_likelihood,
    rollout_for_segment,
    query_text_for_rollout,
):
    n_blk = lax.axis_size("blk")
    blk_index = lax.axis_index("blk")
    rows, width = acceptance_vector.shape
    local_attention_groups = width // GROUP_DIMENSION
    sub = 16
    nsub = rows // sub
    highest = lax.Precision.HIGHEST

    def split(a):
        return (
            a.astype(jnp.float32)
            .reshape(nsub, sub, local_attention_groups, GROUP_DIMENSION)
            .transpose(0, 2, 1, 3)
        )

    inherited_memory = split(acceptance_vector)
    lookup_vectors = split(lookup_vector_array)
    vals = split(payload_vector_array)
    log_decay = -jnp.exp(split(raw_forgetting_rate))
    inclusive = jnp.cumsum(log_decay, axis=2)
    exclusive = inclusive - log_decay
    last = inclusive[:, :, -1, :]
    this_seq = rollout_for_segment[blk_index]
    prev_seq = rollout_for_segment[jnp.maximum(blk_index - 1, 0)]
    starts = jnp.logical_or(blk_index == 0, this_seq != prev_seq).astype(jnp.float32)
    prompt = (
        memory_following_query[query_text_for_rollout[this_seq]]
        .astype(jnp.float32)
        .reshape(local_attention_groups, GROUP_DIMENSION, GROUP_DIMENSION)
    )
    later = jnp.arange(sub)[:, None] > jnp.arange(sub)[None, :]
    spread = exclusive[:, :, :, None, :] - inclusive[:, :, None, :, :]
    weights = jnp.where(later[None, None, :, :, None], jnp.exp(jnp.minimum(spread, 0.0)), 0.0)
    scores = jnp.sum(
        inherited_memory[:, :, :, None, :] * lookup_vectors[:, :, None, :, :] * weights, axis=-1
    )
    group_current_reward = current_reward_vector.reshape(local_attention_groups, GROUP_DIMENSION)
    diagonal_term = jnp.sum(
        inherited_memory * lookup_vectors * group_current_reward[None, :, None, :], axis=-1
    )
    wkv = (
        jnp.einsum("nhts,nhsj->nhtj", scores, vals, precision=highest)
        + diagonal_term[..., None] * vals
    )
    keys_late = lookup_vectors * jnp.exp(last[:, :, None, :] - inclusive)
    delta = jnp.einsum("nhsi,nhsj->nhij", keys_late, vals, precision=highest)

    def advance(state, item):
        change, fall = item
        return (jnp.exp(fall)[:, :, None] * state + change, state)

    end_state, entering = lax.scan(advance, starts * prompt, (delta, last))
    wkv = wkv + jnp.einsum(
        "nhti,nhij->nhtj", inherited_memory * jnp.exp(exclusive), entering, precision=highest
    )
    block_fall = jnp.exp(jnp.sum(last, axis=0)) * (1.0 - starts)

    def handed(fall, state, steps):
        got = passed_along((fall, state.astype(jnp.bfloat16)), "blk", steps)
        return got[0], got[1].astype(jnp.float32)

    fall, incoming = handed(block_fall, end_state, 1)
    covered = 1
    while covered < n_blk // 2 - 1:
        fall_before, state_before = handed(fall, incoming, covered)
        incoming = fall[:, :, None] * state_before + incoming
        fall = fall * fall_before
        covered *= 2
    offsets = jnp.cumsum(last, axis=0) - last
    carried = inherited_memory * jnp.exp(exclusive + offsets[:, :, None, :])
    wkv = wkv + (1.0 - starts) * jnp.einsum("nhti,hij->nhtj", carried, incoming, precision=highest)
    mean = jnp.mean(wkv, axis=-1, keepdims=True)
    var = jnp.mean((wkv - mean) ** 2, axis=-1, keepdims=True)
    normal_h = (wkv - mean) / jnp.sqrt(var + 0.00064)
    normal_h = normal_h.transpose(0, 2, 1, 3).reshape(rows, width) * group_layernorm_scaling
    mixed = (normal_h * jax.nn.silu(raw_gating_signal.astype(jnp.float32))).astype(jnp.bfloat16)
    partial_out = jnp.dot(
        mixed,
        lax.all_gather(closing_projection, "blk", axis=1, tiled=True),
        preferred_element_type=jnp.float32,
    )
    own_rows = lax.psum_scatter(partial_out, "head", scatter_dimension=0, tiled=True)
    hidden = skip_stream_input.astype(jnp.float32) + own_rows
    hmean = jnp.mean(hidden, axis=-1, keepdims=True)
    hvar = jnp.mean((hidden - hmean) ** 2, axis=-1, keepdims=True)
    normed = ((hidden - hmean) / jnp.sqrt(hvar + 1e-05) * closing_layernorm_scaling).astype(
        jnp.bfloat16
    )
    local_rows = normed.shape[0]
    seq_count = query_text_for_rollout.shape[0]
    if n_blk % 4 == 0 and local_rows % 32 == 0 and seq_count <= 128:
        return readout(
            normed,
            vocabulary_readout,
            following_labels,
            response_indicator,
            baseline_logarithmic_likelihood,
            this_seq,
            seq_count,
        )
    vocab_local = vocabulary_readout.shape[0]
    vocab_base = blk_index * vocab_local
    rows_n = lax.all_gather(normed, "blk", axis=0, tiled=True)
    rows_t = lax.all_gather(following_labels, "blk", axis=0, tiled=True)
    logits = lax.dot_general(
        rows_n, vocabulary_readout, (((1,), (1,)), ((), ())), preferred_element_type=jnp.float32
    )
    top = jnp.max(logits, axis=1)
    grand_sum = jnp.sum(jnp.exp(logits - top[:, None]), axis=1)
    entry = jnp.arange(vocab_local, dtype=jnp.int32)[None, :] + vocab_base
    picked = jnp.sum(jnp.where(entry == rows_t[:, None], logits, 0.0), axis=1)
    top, grand_sum, picked = tuple((new for new in (top, grand_sum, picked)))

    def join(first, second):
        peak = jnp.maximum(first[0], second[0])
        summed = first[1] * jnp.exp(first[0] - peak) + second[1] * jnp.exp(second[0] - peak)
        return (peak, summed, first[2] + second[2])

    top, grand_sum, picked = joined((top, grand_sum, picked), "blk", join)
    logp = picked - top - jnp.log(grand_sum)
    mine = lax.dynamic_slice_in_dim(logp, blk_index * local_rows, local_rows)
    token_ratio = response_indicator.astype(jnp.float32) * (mine - baseline_logarithmic_likelihood)
    marker = (jnp.arange(seq_count, dtype=jnp.int32) == this_seq).astype(jnp.float32)
    partial_seq = marker * (jnp.sum(token_ratio) / TOK_BLK)
    seq_ratio = lax.psum(partial_seq, ("blk", "head"))
    return (token_ratio, seq_ratio)


def solution(mesh):
    placed = (
        P("blk", "head"),
        P("blk", "head"),
        P("blk", "head"),
        P("blk", "head"),
        P("blk", "head"),
        P("head"),
        P(None, "head", None),
        P("head"),
        P(),
        P(("blk", "head"), None),
        P("head", "blk"),
        P("blk", None),
        P(("blk", "head")),
        P(("blk", "head")),
        P(("blk", "head")),
        P(),
        P(),
    )
    return jax.shard_map(
        per_device, mesh=mesh, in_specs=placed, out_specs=(P(("blk", "head")), P()), check_vma=False
    )
```

```python
import functools

import jax
import jax.numpy as jnp
from jax import lax
from jax.experimental import pallas as pl
from jax.experimental.pallas import tpu as pltpu
from jax.sharding import PartitionSpec as P

GROUP_DIMENSION = 64
TOK_BLK = 128

MESH = pl.DeviceIdType.MESH


def remote(src, dst, send_sem, recv_sem, device):
    return pltpu.make_async_remote_copy(
        src_ref=src,
        dst_ref=dst,
        send_sem=send_sem,
        recv_sem=recv_sem,
        device_id=device,
        device_id_type=MESH,
    )


def greet_all(n_blk, n_head, blk, head):
    barrier = pltpu.get_barrier_semaphore()
    total = n_blk * n_head
    me = blk * n_head + head

    @pl.loop(1, total)
    def _(i):
        other = lax.rem(me + i, total)
        pl.semaphore_signal(
            barrier, inc=1, device_id=(other // n_head, lax.rem(other, n_head)), device_id_type=MESH
        )

    pl.semaphore_wait(barrier, total - 1)


def readout_kernel(
    n_blk, n_head, rows, chunk,
    mixed_ref, proj_ref, skip_ref, gain_ref, voc_hbm, lab_ref, ind_ref, base_ref, mark_ref,
    tok_ref, seq_ref,
    mix, leaving, keep, coming, back, hid,
    buf, voc, labs, stats, inbox, part, seqbox,
    mix_send, mix_recv, sib_send, sib_recv, back_send, back_recv, voc_sem, block_send, block_recv, lab_send, lab_recv, stat_send, stat_recv, seq_send, seq_recv,
):
    me = lax.axis_index("blk")
    head = lax.axis_index("head")
    flat = me * n_head + head
    planes = n_blk // 4
    z, pos = me // 4, lax.rem(me, 4)
    px = pos + 1 - 2 * lax.rem(pos, 2)
    py = pos + 2 - 4 * (pos // 2)
    pd = 3 - pos
    half = rows // 2
    load = pltpu.make_async_copy(voc_hbm, voc, voc_sem)
    load.start()
    own = pl.ds(pl.multiple_of(me * rows, rows), rows)
    labs[me] = lab_ref[...]
    for h in (0, 1):
        mix[pl.ds(pl.multiple_of((h * 4 + pos) * rows, rows), rows), :] = mixed_ref[
            h * rows : (h + 1) * rows, :
        ]
    greet_all(n_blk, n_head, me, head)

    target = (z * 4 + px, z * 4 + py, me + 4, me - 4)

    def unit(slot, h, direction):
        where = buf.at[pl.ds(pl.multiple_of(slot * rows + h * half, half), half)]
        return remote(
            where, where, block_send.at[direction, slot * 2 + h], block_recv.at[slot * 2 + h],
            (target[direction], head),
        )

    def arrived(slot, h):
        unit(slot, h, 0).wait_recv()

    def lab_copy(i):
        other = lax.rem(me + i, n_blk)
        return remote(labs.at[me], labs.at[me], lab_send.at[other], lab_recv.at[me], (other, head))

    def mix_unit(q, h, direction):
        where = mix.at[pl.ds(pl.multiple_of((h * 4 + q) * rows, rows), rows)]
        return remote(
            where, where, mix_send.at[direction, q * 2 + h], mix_recv.at[q * 2 + h],
            (target[direction], head),
        )

    for h in (0, 1):
        mix_unit(pos, h, 0).start()
        mix_unit(pos, h, 1).start()

    @pl.loop(1, n_blk)
    def _(i):
        lab_copy(i).start()

    mix_unit(px, 0, 0).wait_recv()
    mix_unit(px, 0, 1).start()
    mix_unit(py, 1, 0).wait_recv()
    mix_unit(py, 1, 0).start()
    for q, h in ((px, 1), (py, 0), (pd, 0), (pd, 1)):
        mix_unit(q, h, 0).wait_recv()
    band = proj_ref.shape[1] // planes

    def product(part, into):
        chosen = mix[pl.ds(pl.multiple_of(part * 4 * rows, 4 * rows), 4 * rows), :]

        @pl.loop(0, planes)
        def _(c):
            columns = pl.ds(pl.multiple_of(c * band, band), band)
            into[:, columns] = jnp.dot(
                chosen, proj_ref[:, columns], preferred_element_type=jnp.float32
            )

    product(1 - head, leaving)
    swap = remote(leaving, coming, sib_send, sib_recv, (me, 1 - head))
    swap.start()
    product(head, keep)
    swap.wait_recv()
    keep[...] = keep[...] + coming[...]

    def back_copy(q):
        return remote(
            keep.at[pl.ds(pl.multiple_of(q * rows, rows), rows)], back.at[pos],
            back_send.at[q], back_recv.at[pos], (z * 4 + q, head),
        )

    for q in (px, py, pd):
        back_copy(q).start()
    back[pos] = keep[pl.ds(pl.multiple_of(pos * rows, rows), rows), :]
    for q in (px, py, pd):
        remote(
            keep.at[pl.ds(0, rows)], back.at[q], back_send.at[q], back_recv.at[q], (z * 4 + q, head)
        ).wait_recv()
    for q in range(4):
        for zs in range(planes):
            columns = slice((zs * 4 + q) * band, (zs * 4 + q + 1) * band)
            hid[:, columns] = skip_ref[:, columns].astype(jnp.float32) + back[q][
                :, zs * band : (zs + 1) * band
            ]
    hidden = hid[...]
    centred = hidden - jnp.mean(hidden, axis=1, keepdims=True)
    spread = jnp.mean(centred * centred, axis=1, keepdims=True)
    buf[own, :] = (centred / jnp.sqrt(spread + 1e-5) * gain_ref[...]).astype(jnp.bfloat16)

    for h in (0, 1):
        unit(me, h, 0).start()
        unit(me, h, 1).start()

        @pl.when(z < planes - 1)
        def _():
            unit(me, h, 2).start()

        @pl.when(z > 0)
        def _():
            unit(me, h, 3).start()

    def at_distance(d, body):
        if d == 0:
            body(z, 0)
            return

        @pl.when(z - d >= 0)
        def _():
            body(z - d, -1)

        @pl.when(z + d < planes)
        def _():
            body(z + d, 1)

    def column(zs, side):
        slot = zs * 4 + pos
        for h in (0, 1):
            arrived(slot, h)

            @pl.when(z < planes - 1 if side < 0 else z > 0)
            def _():
                unit(slot, h, 2 if side < 0 else 3).start()

            unit(slot, h, 0).start()
            unit(slot, h, 1).start()

    def diagonal(zs, side):
        sx, sy = zs * 4 + px, zs * 4 + py
        arrived(sx, 0)
        unit(sx, 0, 1).start()
        arrived(sy, 1)
        unit(sy, 1, 0).start()

    def stat_copy(zs, q):
        other = zs * 4 + q
        return remote(stats.at[zs], inbox.at[me], stat_send.at[other], stat_recv.at[me], (other, head))

    def scores(zs, side):
        arrived(zs * 4 + px, 1)
        arrived(zs * 4 + py, 0)
        arrived(zs * 4 + pd, 0)
        arrived(zs * 4 + pd, 1)
        lab = jnp.zeros((1, 4 * rows), jnp.int32)
        for q in range(4):
            slot = zs * 4 + q

            @pl.when(slot != me)
            def _():
                remote(
                    labs.at[slot], labs.at[slot], lab_send.at[slot], lab_recv.at[slot],
                    (target[0], head),
                ).wait_recv()

        for q in range(4):
            lab = lab + labs[zs * 4 + q][0:1, :]
        tokens = buf[pl.ds(pl.multiple_of(zs * 4 * rows, 4 * rows), 4 * rows), :]
        count = voc.shape[0]
        entry = lax.broadcasted_iota(jnp.int32, (chunk, 4 * rows), 0) + me * count

        def step(c, carry):
            top, total, picked = carry
            part_of = voc[pl.ds(pl.multiple_of(c * chunk, chunk), chunk), :]
            logits = lax.dot_general(
                part_of, tokens, (((1,), (1,)), ((), ())), preferred_element_type=jnp.float32
            )
            peak = jnp.maximum(top, jnp.max(logits, axis=0, keepdims=True))
            total = total * jnp.exp(top - peak) + jnp.sum(
                jnp.exp(logits - peak), axis=0, keepdims=True
            )
            hit = entry + c * chunk == lab
            picked = picked + jnp.sum(jnp.where(hit, logits, 0.0), axis=0, keepdims=True)
            return peak, total, picked

        zero = jnp.zeros((1, 4 * rows), jnp.float32)
        top, total, picked = lax.fori_loop(0, count // chunk, step, (zero - 3.0e38, zero, zero))
        stats[zs, 0:1, :] = top
        stats[zs, 1:2, :] = total
        stats[zs, 2:3, :] = picked
        stats[zs, 3:8, :] = jnp.zeros((5, 4 * rows), jnp.float32)
        for q in range(4):
            if side != 0:
                stat_copy(zs, q).start()
            else:

                @pl.when(q != pos)
                def _():
                    stat_copy(zs, q).start()

    for d in range(planes + 2):
        if 1 <= d < planes:
            at_distance(d, column)
        if d == 2:
            load.wait()
        if 2 <= d:
            at_distance(d - 2, scores)
        if 1 <= d <= planes:
            at_distance(d - 1, diagonal)

    inbox[me] = stats[z]

    def stat_arrival(i):
        other = lax.rem(me + i, n_blk)
        remote(
            stats.at[0], inbox.at[other], stat_send.at[other], stat_recv.at[other], (other, head)
        ).wait_recv()

    pl.loop(1, n_blk)(stat_arrival)
    peak = inbox[0][0:1, :]
    for i in range(1, n_blk):
        peak = jnp.maximum(peak, inbox[i][0:1, :])
    total = jnp.zeros_like(peak)
    picked = jnp.zeros_like(peak)
    for i in range(n_blk):
        total = total + inbox[i][1:2, :] * jnp.exp(inbox[i][0:1, :] - peak)
        picked = picked + inbox[i][2:3, :]
    logp = picked - peak - jnp.log(total)
    ratio = ind_ref[...] * (logp - base_ref[...])
    tok_ref[...] = ratio
    part[...] = mark_ref[...] * (jnp.sum(ratio[0:1, :], axis=1, keepdims=True) / TOK_BLK)
    seqbox[flat] = part[...]
    everyone = n_blk * n_head

    def seq_copy(i):
        other = lax.rem(flat + i, everyone)
        return remote(
            part, seqbox.at[flat], seq_send.at[other], seq_recv.at[flat],
            (other // n_head, lax.rem(other, n_head)),
        )

    @pl.loop(1, everyone)
    def _(i):
        seq_copy(i).start()

    @pl.loop(1, everyone)
    def _(i):
        other = lax.rem(flat + i, everyone)
        remote(
            part, seqbox.at[other], seq_send.at[other], seq_recv.at[other],
            (other // n_head, lax.rem(other, n_head)),
        ).wait_recv()

    summed = seqbox[0]
    for i in range(1, everyone):
        summed = summed + seqbox[i]
    seq_ref[...] = summed

    for h in (0, 1):
        mix_unit(pos, h, 0).wait_send()
        mix_unit(pos, h, 1).wait_send()
    mix_unit(px, 0, 1).wait_send()
    mix_unit(py, 1, 0).wait_send()
    swap.wait_send()
    for q in (px, py, pd):
        back_copy(q).wait_send()

    @pl.loop(1, everyone)
    def _(i):
        seq_copy(i).wait_send()

    @pl.loop(1, n_blk)
    def _(i):
        lab_copy(i).wait_send()
        other = lax.rem(me + i, n_blk)
        remote(
            stats.at[other // 4], inbox.at[me], stat_send.at[other], stat_recv.at[me], (other, head)
        ).wait_send()

    for h in (0, 1):
        unit(me, h, 0).wait_send()
        unit(me, h, 1).wait_send()

        @pl.when(z < planes - 1)
        def _():
            unit(me, h, 2).wait_send()

        @pl.when(z > 0)
        def _():
            unit(me, h, 3).wait_send()

    def column_sent(zs, side):
        slot = zs * 4 + pos
        for h in (0, 1):

            @pl.when(z < planes - 1 if side < 0 else z > 0)
            def _():
                unit(slot, h, 2 if side < 0 else 3).wait_send()

            unit(slot, h, 0).wait_send()
            unit(slot, h, 1).wait_send()

    def diagonal_sent(zs, side):
        unit(zs * 4 + px, 0, 1).wait_send()
        unit(zs * 4 + py, 1, 0).wait_send()

    for d in range(planes):
        if d > 0:
            at_distance(d, column_sent)
        at_distance(d, diagonal_sent)


def readout(mixed, projection, skip, gain, vocabulary, labels, indicator, baseline, this_seq, seq_count):
    n_blk, n_head = lax.axis_size("blk"), lax.axis_size("head")
    rows, width = skip.shape
    columns = projection.shape[1]
    count = vocabulary.shape[0]
    pos = lax.axis_index("blk") % 4

    def placed(a):
        spot = jnp.arange(4)[:, None] == pos
        lane = jnp.where(spot, a[None, :], jnp.zeros((), a.dtype)).reshape(1, 4 * rows)
        return jnp.broadcast_to(lane, (8, 4 * rows))

    mark = jnp.broadcast_to((jnp.arange(128)[None, :] == this_seq).astype(jnp.float32), (8, 128))
    dma = pltpu.SemaphoreType.DMA
    vmem = pl.BlockSpec(memory_space=pltpu.VMEM)
    tok, seq = pl.pallas_call(
        functools.partial(readout_kernel, n_blk, n_head, rows, min(512, count)),
        out_shape=(
            jax.ShapeDtypeStruct((8, 4 * rows), jnp.float32),
            jax.ShapeDtypeStruct((8, 128), jnp.float32),
        ),
        in_specs=[vmem] * 4 + [pl.BlockSpec(memory_space=pl.ANY)] + [vmem] * 4,
        out_specs=(vmem, vmem),
        scratch_shapes=[
            pltpu.VMEM((8 * rows, mixed.shape[1]), jnp.bfloat16),
            pltpu.VMEM((4 * rows, columns), jnp.float32),
            pltpu.VMEM((4 * rows, columns), jnp.float32),
            pltpu.VMEM((4 * rows, columns), jnp.float32),
            pltpu.VMEM((4, rows, columns), jnp.float32),
            pltpu.VMEM((rows, width), jnp.float32),
            pltpu.VMEM((n_blk * rows, width), jnp.bfloat16),
            pltpu.VMEM((count, width), jnp.bfloat16),
            pltpu.VMEM((n_blk, 8, 4 * rows), jnp.int32),
            pltpu.VMEM((n_blk // 4, 8, 4 * rows), jnp.float32),
            pltpu.VMEM((n_blk, 8, 4 * rows), jnp.float32),
            pltpu.VMEM((8, 128), jnp.float32),
            pltpu.VMEM((n_blk * n_head, 8, 128), jnp.float32),
            dma((2, 8)),
            dma((8,)),
            dma,
            dma,
            dma((4,)),
            dma((4,)),
            dma,
            dma((4, 2 * n_blk)),
            dma((2 * n_blk,)),
            dma((n_blk,)),
            dma((n_blk,)),
            dma((n_blk,)),
            dma((n_blk,)),
            dma((n_blk * n_head,)),
            dma((n_blk * n_head,)),
        ],
        compiler_params=pltpu.CompilerParams(
            collective_id=1, has_side_effects=True, vmem_limit_bytes=48 * 2**20
        ),
        cost_estimate=pl.CostEstimate(
            flops=2 * n_blk * rows * width * count,
            bytes_accessed=2 * count * width,
            transcendentals=n_blk * rows * count,
        ),
    )(
        mixed,
        projection,
        skip,
        gain.reshape(1, width),
        vocabulary,
        placed(labels),
        placed(indicator.astype(jnp.float32)),
        placed(baseline),
        mark,
    )
    return lax.dynamic_slice_in_dim(tok[0], pos * rows, rows), seq[0, :seq_count]


def halves(a):
    high = a.astype(jnp.bfloat16)
    return high, (a - high.astype(jnp.float32)).astype(jnp.bfloat16)


def product32(a, b, dims):
    return lax.dot_general(a, b, (dims, ((), ())), preferred_element_type=jnp.float32)


def across(a, b):
    ah, al = halves(a)
    bh, bl = halves(b)
    return product32(
        jnp.concatenate([ah, ah, al], axis=1), jnp.concatenate([bh, bl, bh], axis=1), ((1,), (1,))
    )


def times_exact(a, b):
    return product32(
        jnp.concatenate(halves(a), axis=1), jnp.concatenate([b, b], axis=0), ((1,), (0,))
    )


def memory_kernel(
    n_blk, n_head,
    r_ref, k_ref, v_ref, g_ref, w_ref, u_ref, gain_ref, prompt_ref, first_ref,
    mixed_ref,
    incl, wk, leaf, fall, agg, aggfall, enter,
    leaf_send, leaf_recv, fall_send, fall_recv, agg_send, agg_recv, aggfall_send, aggfall_recv,
):
    me = lax.axis_index("blk")
    head = lax.axis_index("head")
    z, pos = me // 4, lax.rem(me, 4)
    planes = n_blk // 4
    px = pos + 1 - 2 * lax.rem(pos, 2)
    py = pos + 2 - 4 * (pos // 2)
    pd = 3 - pos
    tokens, width = r_ref.shape
    pairs = width // 128
    dim = GROUP_DIMENSION
    sub = 32
    barrier = pltpu.get_barrier_semaphore()

    @pl.loop(1, n_blk)
    def _(i):
        pl.semaphore_signal(
            barrier, inc=1, device_id=(lax.rem(me + i, n_blk), head), device_id_type=MESH
        )

    lane = lax.broadcasted_iota(jnp.int32, (dim, 128), 1) < dim
    wide_lane = lax.broadcasted_iota(jnp.int32, (tokens, 128), 1) < dim
    line = lax.broadcasted_iota(jnp.int32, (tokens, tokens), 0)
    column = lax.broadcasted_iota(jnp.int32, (tokens, tokens), 1)
    tri = jnp.where(line >= column, 1.0, 0.0).astype(jnp.bfloat16)
    same_head = jnp.where(line // dim == column // dim, 1.0, 0.0).astype(jnp.bfloat16)
    first = first_ref[0:1, :]

    def lanes_of(p):
        return pl.ds(pl.multiple_of(p * 128, 128), 128)

    def state_of(p):
        return pl.ds(pl.multiple_of(p * dim, dim), dim)

    def f32(ref, lanes):
        return ref[:, lanes].astype(jnp.float32)

    @pl.loop(0, pairs)
    def _(p):
        lanes = lanes_of(p)
        log_decay = -jnp.exp(f32(w_ref, lanes))
        high, low = halves(log_decay)
        rest = (log_decay - high.astype(jnp.float32) - low.astype(jnp.float32)).astype(jnp.bfloat16)
        upto = product32(
            jnp.concatenate([tri, tri, tri], axis=1),
            jnp.concatenate([high, low, rest], axis=0),
            ((1,), (0,)),
        )
        incl[:, lanes] = upto
        total = upto[tokens - 1 : tokens, :]
        kh, kl = halves(f32(k_ref, lanes) * jnp.exp(total - upto))
        v = v_ref[:, lanes]
        change = product32(
            jnp.concatenate([v, v], axis=0), jnp.concatenate([kh, kl], axis=0), ((0,), (0,))
        )
        change = jnp.where(lane, change[:dim], change[dim:])
        shrink = jnp.exp(total)
        prompt = prompt_ref[state_of(p), :].astype(jnp.float32)
        leaf[pos, state_of(p), :] = (change + first * (shrink * prompt)).astype(jnp.bfloat16)
        fall[pos, pl.ds(p, 1), :] = shrink * (1.0 - first)

    pl.semaphore_wait(barrier, n_blk - 1)

    def leaf_copies(q, slot):
        device = (z * 4 + q, head)
        return (
            remote(leaf.at[slot], leaf.at[slot], leaf_send.at[q], leaf_recv.at[slot], device),
            remote(fall.at[slot], fall.at[slot], fall_send.at[q], fall_recv.at[slot], device),
        )

    def agg_copies(d):
        device = (me + 4 * d, head)
        return (
            remote(agg.at[0], agg.at[d], agg_send.at[d], agg_recv.at[d], device),
            remote(aggfall.at[0], aggfall.at[d], aggfall_send.at[d], aggfall_recv.at[d], device),
        )

    for q in (px, py, pd):
        for copy in leaf_copies(q, pos):
            copy.start()

    def inner(p):
        lanes = lanes_of(p)
        upto = incl[:, lanes]
        before = upto + jnp.exp(f32(w_ref, lanes))
        r = f32(r_ref, lanes)
        k = f32(k_ref, lanes)
        v = v_ref[:, lanes]
        own = times_exact(r * k * u_ref[:, lanes], same_head) * v.astype(jnp.float32)
        for c in range(tokens // sub):
            these = slice(c * sub, (c + 1) * sub)
            middle = upto[c * sub + sub // 2 - 1 : c * sub + sub // 2, :]
            rc = r[these] * jnp.exp(before[these] - middle)
            kc = k * jnp.exp(jnp.minimum(middle - upto, 44.0))
            pick = wide_lane[:sub]
            rows = jnp.concatenate(
                [jnp.where(pick, rc, 0.0), jnp.where(pick, 0.0, rc)], axis=0
            )
            scores = across(rows, kc)
            at = lax.broadcasted_iota(jnp.int32, (2 * sub, tokens), 0) % sub + c * sub
            source = lax.broadcasted_iota(jnp.int32, (2 * sub, tokens), 1)
            out = times_exact(jnp.where(at > source, scores, 0.0), v)
            wk[these, lanes] = own[these] + jnp.where(pick, out[:sub], out[sub:])

    quarter = pairs // 4
    pl.loop(0, quarter)(inner)
    for q in (px, py, pd):
        for copy in leaf_copies(q, q):
            copy.wait_recv()

    @pl.loop(0, pairs)
    def _(p):
        where = state_of(p)
        state = leaf[0, where, :].astype(jnp.float32)
        shrink = fall[0, pl.ds(p, 1), :]
        for q in range(1, 4):
            factor = fall[q, pl.ds(p, 1), :]
            state = leaf[q, where, :].astype(jnp.float32) + factor * state
            shrink = factor * shrink
        agg[0, where, :] = state.astype(jnp.bfloat16)
        aggfall[0, pl.ds(p, 1), :] = shrink

    for d in (1, 2):

        @pl.when(z + d < planes)
        def _():
            for copy in agg_copies(d):
                copy.start()

    pl.loop(quarter, pairs)(inner)

    for d in (1, 2):

        @pl.when(z - d >= 0)
        def _():
            for copy in agg_copies(d):
                copy.wait_recv()

        @pl.when(z - d < 0)
        def _():
            agg[d] = jnp.zeros(agg.shape[1:], agg.dtype)
            aggfall[d] = jnp.zeros(aggfall.shape[1:], aggfall.dtype)

    @pl.loop(0, pairs)
    def _(p):
        where = state_of(p)
        state = agg[1, where, :].astype(jnp.float32) + aggfall[1, pl.ds(p, 1), :] * agg[
            2, where, :
        ].astype(jnp.float32)
        for q in range(3):
            later = leaf[q, where, :].astype(jnp.float32) + fall[q, pl.ds(p, 1), :] * state
            state = jnp.where(pos > q, later, state)
        state = jnp.where(first > 0.0, prompt_ref[where, :].astype(jnp.float32), state)
        lanes = lanes_of(p)
        before = incl[:, lanes] + jnp.exp(f32(w_ref, lanes))
        spread = jnp.concatenate([jnp.where(lane, state, 0.0), jnp.where(lane, 0.0, state)], axis=0)
        out = wk[:, lanes] + across(f32(r_ref, lanes) * jnp.exp(before), spread)
        centred = out - times_exact(out, same_head) * (1.0 / dim)
        var = times_exact(centred * centred, same_head) * (1.0 / dim)
        gate = f32(g_ref, lanes)
        normal = centred / jnp.sqrt(var + 0.00064) * gain_ref[:, lanes]
        mixed_ref[:, lanes] = (normal * (gate / (1.0 + jnp.exp(-gate)))).astype(jnp.bfloat16)

    for q in (px, py, pd):
        for copy in leaf_copies(q, pos):
            copy.wait_send()
    for d in (1, 2):

        @pl.when(z + d < planes)
        def _():
            for copy in agg_copies(d):
                copy.wait_send()


def mixed_rows(r, k, v, g, w, u, gain, prompt, starts):
    n_blk, n_head = lax.axis_size("blk"), lax.axis_size("head")
    tokens, width = r.shape
    dim = GROUP_DIMENSION
    pairs = width // 128
    turned = prompt.reshape(pairs, 2, dim, dim).transpose(0, 3, 1, 2).reshape(pairs * dim, 128)
    dma = pltpu.SemaphoreType.DMA
    vmem = pl.BlockSpec(memory_space=pltpu.VMEM)
    return pl.pallas_call(
        functools.partial(memory_kernel, n_blk, n_head),
        out_shape=jax.ShapeDtypeStruct((tokens, width), jnp.bfloat16),
        in_specs=[vmem] * 9,
        out_specs=vmem,
        scratch_shapes=[
            pltpu.VMEM((tokens, width), jnp.float32),
            pltpu.VMEM((tokens, width), jnp.float32),
            pltpu.VMEM((4, pairs * dim, 128), jnp.bfloat16),
            pltpu.VMEM((4, pairs, 128), jnp.float32),
            pltpu.VMEM((3, pairs * dim, 128), jnp.bfloat16),
            pltpu.VMEM((3, pairs, 128), jnp.float32),
            pltpu.VMEM((8, 128), jnp.float32),
        ]
        + [dma((4,))] * 8,
        compiler_params=pltpu.CompilerParams(
            collective_id=2, has_side_effects=True, vmem_limit_bytes=32 * 2**20
        ),
        cost_estimate=pl.CostEstimate(
            flops=80 * tokens * width * 128, bytes_accessed=12 * tokens * width,
            transcendentals=8 * tokens * width,
        ),
    )(r, k, v, g, w, u.reshape(1, width), gain.reshape(1, width), turned,
      jnp.broadcast_to(starts, (8, 128)))


def passed_along(value, axis, steps):
    count = lax.axis_size(axis)
    first, last = (max(0, -steps), min(count, count - steps))
    pairs = [(source, source + steps) for source in range(first, last)]
    return jax.tree.map(lambda a: lax.ppermute(a, axis, pairs), value)


def joined(part, axis, combine):
    gathered = jax.tree.map(lambda a: lax.all_gather(a, axis), part)

    def take(source):
        return jax.tree.map(lambda a: lax.dynamic_index_in_dim(a, source, 0, False), gathered)

    return lax.fori_loop(
        1, lax.axis_size(axis), lambda source, state: combine(state, take(source)), take(0)
    )


def per_device(
    acceptance_vector,
    lookup_vector_array,
    payload_vector_array,
    raw_gating_signal,
    raw_forgetting_rate,
    current_reward_vector,
    memory_following_query,
    group_layernorm_scaling,
    closing_layernorm_scaling,
    skip_stream_input,
    closing_projection,
    vocabulary_readout,
    following_labels,
    response_indicator,
    baseline_logarithmic_likelihood,
    rollout_for_segment,
    query_text_for_rollout,
):
    n_blk = lax.axis_size("blk")
    blk_index = lax.axis_index("blk")
    rows, width = acceptance_vector.shape
    local_attention_groups = width // GROUP_DIMENSION
    sub = 16
    nsub = rows // sub
    highest = lax.Precision.HIGHEST
    seq_count = query_text_for_rollout.shape[0]
    local_rows = skip_stream_input.shape[0]
    if (
        n_blk % 4 == 0
        and n_blk // 2 <= 8
        and lax.axis_size("head") == 2
        and rows == 2 * local_rows
        and local_rows % 32 == 0
        and rows == 128
        and width % 512 == 0
        and seq_count <= 128
    ):
        columns = [[z * 4 + at for z in range(n_blk // 4)] for at in range(4)]
        projection = lax.all_gather(
            closing_projection, "blk", axis=1, tiled=True, axis_index_groups=columns
        )
        this_seq = rollout_for_segment[blk_index]
        prev_seq = rollout_for_segment[jnp.maximum(blk_index - 1, 0)]
        starts = jnp.logical_or(blk_index == 0, this_seq != prev_seq).astype(jnp.float32)
        mixed = mixed_rows(
            acceptance_vector,
            lookup_vector_array,
            payload_vector_array,
            raw_gating_signal,
            raw_forgetting_rate,
            current_reward_vector,
            group_layernorm_scaling,
            memory_following_query[query_text_for_rollout[this_seq]],
            starts,
        )
        return readout(
            mixed,
            projection,
            skip_stream_input,
            closing_layernorm_scaling,
            vocabulary_readout,
            following_labels,
            response_indicator,
            baseline_logarithmic_likelihood,
            this_seq,
            seq_count,
        )

    def split(a):
        return (
            a.astype(jnp.float32)
            .reshape(nsub, sub, local_attention_groups, GROUP_DIMENSION)
            .transpose(0, 2, 1, 3)
        )

    inherited_memory = split(acceptance_vector)
    lookup_vectors = split(lookup_vector_array)
    vals = split(payload_vector_array)
    log_decay = -jnp.exp(split(raw_forgetting_rate))
    inclusive = jnp.cumsum(log_decay, axis=2)
    exclusive = inclusive - log_decay
    last = inclusive[:, :, -1, :]
    this_seq = rollout_for_segment[blk_index]
    prev_seq = rollout_for_segment[jnp.maximum(blk_index - 1, 0)]
    starts = jnp.logical_or(blk_index == 0, this_seq != prev_seq).astype(jnp.float32)
    prompt = (
        memory_following_query[query_text_for_rollout[this_seq]]
        .astype(jnp.float32)
        .reshape(local_attention_groups, GROUP_DIMENSION, GROUP_DIMENSION)
    )
    later = jnp.arange(sub)[:, None] > jnp.arange(sub)[None, :]
    spread = exclusive[:, :, :, None, :] - inclusive[:, :, None, :, :]
    weights = jnp.where(later[None, None, :, :, None], jnp.exp(jnp.minimum(spread, 0.0)), 0.0)
    scores = jnp.sum(
        inherited_memory[:, :, :, None, :] * lookup_vectors[:, :, None, :, :] * weights, axis=-1
    )
    group_current_reward = current_reward_vector.reshape(local_attention_groups, GROUP_DIMENSION)
    diagonal_term = jnp.sum(
        inherited_memory * lookup_vectors * group_current_reward[None, :, None, :], axis=-1
    )
    wkv = (
        jnp.einsum("nhts,nhsj->nhtj", scores, vals, precision=highest)
        + diagonal_term[..., None] * vals
    )
    keys_late = lookup_vectors * jnp.exp(last[:, :, None, :] - inclusive)
    delta = jnp.einsum("nhsi,nhsj->nhij", keys_late, vals, precision=highest)

    def advance(state, item):
        change, fall = item
        return (jnp.exp(fall)[:, :, None] * state + change, state)

    end_state, entering = lax.scan(advance, starts * prompt, (delta, last))
    wkv = wkv + jnp.einsum(
        "nhti,nhij->nhtj", inherited_memory * jnp.exp(exclusive), entering, precision=highest
    )
    block_fall = jnp.exp(jnp.sum(last, axis=0)) * (1.0 - starts)

    def handed(fall, state, steps):
        got = passed_along((fall, state.astype(jnp.bfloat16)), "blk", steps)
        return got[0], got[1].astype(jnp.float32)

    fall, incoming = handed(block_fall, end_state, 1)
    covered = 1
    while covered < n_blk // 2 - 1:
        fall_before, state_before = handed(fall, incoming, covered)
        incoming = fall[:, :, None] * state_before + incoming
        fall = fall * fall_before
        covered *= 2
    offsets = jnp.cumsum(last, axis=0) - last
    carried = inherited_memory * jnp.exp(exclusive + offsets[:, :, None, :])
    wkv = wkv + (1.0 - starts) * jnp.einsum("nhti,hij->nhtj", carried, incoming, precision=highest)
    mean = jnp.mean(wkv, axis=-1, keepdims=True)
    var = jnp.mean((wkv - mean) ** 2, axis=-1, keepdims=True)
    normal_h = (wkv - mean) / jnp.sqrt(var + 0.00064)
    normal_h = normal_h.transpose(0, 2, 1, 3).reshape(rows, width) * group_layernorm_scaling
    mixed = (normal_h * jax.nn.silu(raw_gating_signal.astype(jnp.float32))).astype(jnp.bfloat16)
    partial_out = jnp.dot(
        mixed,
        lax.all_gather(closing_projection, "blk", axis=1, tiled=True),
        preferred_element_type=jnp.float32,
    )
    own_rows = lax.psum_scatter(partial_out, "head", scatter_dimension=0, tiled=True)
    hidden = skip_stream_input.astype(jnp.float32) + own_rows
    hmean = jnp.mean(hidden, axis=-1, keepdims=True)
    hvar = jnp.mean((hidden - hmean) ** 2, axis=-1, keepdims=True)
    normed = ((hidden - hmean) / jnp.sqrt(hvar + 1e-05) * closing_layernorm_scaling).astype(
        jnp.bfloat16
    )
    vocab_local = vocabulary_readout.shape[0]
    vocab_base = blk_index * vocab_local
    rows_n = lax.all_gather(normed, "blk", axis=0, tiled=True)
    rows_t = lax.all_gather(following_labels, "blk", axis=0, tiled=True)
    logits = lax.dot_general(
        rows_n, vocabulary_readout, (((1,), (1,)), ((), ())), preferred_element_type=jnp.float32
    )
    top = jnp.max(logits, axis=1)
    grand_sum = jnp.sum(jnp.exp(logits - top[:, None]), axis=1)
    entry = jnp.arange(vocab_local, dtype=jnp.int32)[None, :] + vocab_base
    picked = jnp.sum(jnp.where(entry == rows_t[:, None], logits, 0.0), axis=1)
    top, grand_sum, picked = tuple((new for new in (top, grand_sum, picked)))

    def join(first, second):
        peak = jnp.maximum(first[0], second[0])
        summed = first[1] * jnp.exp(first[0] - peak) + second[1] * jnp.exp(second[0] - peak)
        return (peak, summed, first[2] + second[2])

    top, grand_sum, picked = joined((top, grand_sum, picked), "blk", join)
    logp = picked - top - jnp.log(grand_sum)
    mine = lax.dynamic_slice_in_dim(logp, blk_index * local_rows, local_rows)
    token_ratio = response_indicator.astype(jnp.float32) * (mine - baseline_logarithmic_likelihood)
    seq_count = query_text_for_rollout.shape[0]
    marker = (jnp.arange(seq_count, dtype=jnp.int32) == this_seq).astype(jnp.float32)
    partial_seq = marker * (jnp.sum(token_ratio) / TOK_BLK)
    seq_ratio = lax.psum(partial_seq, ("blk", "head"))
    return (token_ratio, seq_ratio)


def solution(mesh):
    placed = (
        P("blk", "head"),
        P("blk", "head"),
        P("blk", "head"),
        P("blk", "head"),
        P("blk", "head"),
        P("head"),
        P(None, "head", None),
        P("head"),
        P(),
        P(("blk", "head"), None),
        P("head", "blk"),
        P("blk", None),
        P(("blk", "head")),
        P(("blk", "head")),
        P(("blk", "head")),
        P(),
        P(),
    )
    return jax.shard_map(
        per_device, mesh=mesh, in_specs=placed, out_specs=(P(("blk", "head")), P()), check_vma=False
    )
```
